32 devices in a mesh: dp: 8 (over y, x, core), expert: 4 (over z).
Axes of the slice: x: 2, y: 2, z: 4, core: 2. Of those that a mesh axis runs over, the one named last changes fastest.
Arguments:
- tokens: bfloat16 [4096, 1024], P(('dp', 'expert')), may hold values from -6 to 6
- routing: int32 [4096, 2], P(('dp', 'expert')), may hold values from 0 to 3, as said below
- combine: float32 [4096, 2], P(('dp', 'expert')), may hold values from 0.1 to 1
- upstream: bfloat16 [4096, 1024], P(('dp', 'expert')), may hold values from -6 to 6
- gate_weight: bfloat16 [4, 1024, 384], P('expert', 'dp'), may hold values from -0.1875 to 0.1875
- up_weight: bfloat16 [4, 1024, 384], P('expert', 'dp'), may hold values from -0.1875 to 0.1875
- down_weight: bfloat16 [4, 1024, 384], P('expert', 'dp'), may hold values from -0.3125 to 0.3125
Outputs:
- layer_output: bfloat16 [4096, 1024], P(('dp', 'expert'))
- token_grad: bfloat16 [4096, 1024], P(('dp', 'expert'))
- combine_grad: float32 [4096, 2], P(('dp', 'expert'))
- gate_grad: float32 [4, 1024, 384], P('expert', 'dp')
- up_grad: float32 [4, 1024, 384], P('expert', 'dp')
The draws below stay inside these ranges and needn't reach their ends.
Inputs may be any that keep to these rules, and one draw needn't show every extreme that they name: `routing`: each row names 2 different experts. The rows fall into blocks of 128 (the rows of one device), and 4 consecutive blocks form a data group. In each data group one expert, the group's hot expert, is named by exactly 96 rows of every block of the group; a second expert of the group is named by exactly 64 rows of every block of the group; every other expert is named by at most 64 rows of a block.
All inputs are finite; a program needn't handle non-finite values.
Results may differ from the reference program's by a relative error of at most 0.0065.
Values may be sent and summed in bfloat16 or wider, within the bound.
A program may use at most 64 MiB of HBM per device.

```python
import math
import jax
import jax.numpy as jnp
from jax import lax

D = 1024
F = 384
TOP = 2
TOK_DEV = 128
EXPERTS = 4
GROUPS = 8
TOKENS = 4096
CAP = 96
COLD = 64


def route_block(block_key, hot_id, second_id):
    order_key, token_key, swap_key = jax.random.split(block_key, 3)
    slot_total = (EXPERTS - 1) * COLD
    needed = TOP * TOK_DEV - CAP
    cold_list = jnp.arange(EXPERTS - 1, dtype=jnp.int32)
    cold_list = jnp.where(cold_list < hot_id, cold_list, cold_list + 1)
    second_place = second_id - (second_id > hot_id).astype(jnp.int32)
    slot_ids = jnp.arange(slot_total, dtype=jnp.int32)
    priority = jax.random.permutation(order_key, slot_total).astype(jnp.int32)
    priority = jnp.where(slot_ids // COLD == second_place, -1 - slot_ids, priority)
    chosen = jnp.sort(jnp.argsort(priority)[:needed])
    cold_picks = cold_list[chosen // COLD]
    sequence = jnp.concatenate([jnp.full((CAP,), hot_id, jnp.int32), cold_picks.astype(jnp.int32)])
    first_pick = sequence[:TOK_DEV]
    second_pick = sequence[TOK_DEV:]
    swap_bits = jax.random.randint(swap_key, (TOK_DEV,), 0, 2)
    left_pick = jnp.where(swap_bits == 1, second_pick, first_pick)
    right_pick = jnp.where(swap_bits == 1, first_pick, second_pick)
    pick_pairs = jnp.stack([left_pick, right_pick], axis=1)
    return pick_pairs[jax.random.permutation(token_key, TOK_DEV)]


def draw_routing(key, part):
    group_count = TOKENS // (TOK_DEV * EXPERTS)
    block_count = group_count * EXPERTS
    hot_key, second_key, block_key = jax.random.split(jax.random.fold_in(key, 17), 3)
    hot_ids = jax.random.randint(hot_key, (group_count,), 0, EXPERTS).astype(jnp.int32)
    second_ids = ((hot_ids + jax.random.randint(second_key, (group_count,), 1, EXPERTS)) % EXPERTS).astype(jnp.int32)
    block_keys = jax.random.split(block_key, block_count)
    block_rows = jax.vmap(route_block)(block_keys, jnp.repeat(hot_ids, EXPERTS), jnp.repeat(second_ids, EXPERTS))
    return block_rows.reshape(TOKENS, TOP).astype(jnp.int32)


def strengthened(array, stream_key, source, target, parts, factor):
    owner, partner = [(jnp.arange(array.shape[dim]) // (array.shape[dim] // parts)).reshape([-1 if axis == dim else 1 for axis in range(array.ndim)]) for dim in (source, target)]
    chosen = jax.random.permutation(stream_key, parts)[partner]
    strong = (owner == chosen) | (owner == (partner + parts // 2) % parts)
    return jnp.where(strong, factor * array, array)


def block_scale(key, extent, cuts, least, largest):
    factor_of = 1.0
    for dim, parts in cuts:
        steps = jax.random.uniform(jax.random.fold_in(jax.random.fold_in(key, 6), dim), (parts,), jnp.float32, least / len(cuts), largest / len(cuts))
        factor_of = factor_of * jnp.repeat(jnp.exp(steps), extent[dim] // parts).reshape((-1,) + (1,) * (len(extent) - 1 - dim))
    return factor_of


def gaussian(own_key, extent, deviation, reach, cuts=(), kind=jnp.bfloat16):
    values = deviation * jax.random.normal(own_key, extent, jnp.float32)
    if cuts:
        values = values * block_scale(own_key, extent, cuts, -0.22, 0.18)
    return jnp.clip(values, -reach, reach).astype(kind)


def noise_with(own_key, shape, width, limit, cuts, heavy, kind=jnp.bfloat16):
    result = width * jax.random.normal(own_key, shape, jnp.float32)
    if cuts:
        result = result * block_scale(own_key, shape, cuts, -0.22, 0.18)
    return jnp.clip(strengthened(result, jax.random.fold_in(own_key, 3), *heavy), -limit, limit).astype(kind)


def setup_inputs(seed: int = 0) -> dict:
    arg_keys = jax.random.split(jax.random.key(seed), 8)
    tokens = noise_with(arg_keys[0], (TOKENS, D), 1.0, 6.0, ((0, 32),), (0, 1, 32, 2.75))
    routing = draw_routing(jax.random.fold_in(arg_keys[7], 71), 0)
    combine = jnp.clip(jnp.exp(math.log(1.0) - 2.3025851 * jax.random.uniform(arg_keys[2], (TOKENS, TOP), jnp.float32) ** block_scale(arg_keys[2], (TOKENS, TOP), ((0, 32),), -0.2, 0.2)), 0.1, 1.0)
    upstream = gaussian(arg_keys[3], (TOKENS, D), 1.0, 6.0, ((0, 32),))
    gate_weight = gaussian(arg_keys[4], (EXPERTS, D, F), D ** -0.5, 0.1875, ((0, 4), (1, 8)))
    up_weight = gaussian(arg_keys[5], (EXPERTS, D, F), D ** -0.5, 0.1875, ((0, 4), (1, 8)))
    down_weight = gaussian(arg_keys[6], (EXPERTS, D, F), F ** -0.5, 0.3125, ((0, 4), (1, 8)))
    return {"tokens": tokens, "routing": routing, "combine": combine, "upstream": upstream, "gate_weight": gate_weight, "up_weight": up_weight, "down_weight": down_weight}


def narrow(values):
    return lax.optimization_barrier(values.astype(jnp.bfloat16))


def reference(tokens, routing, combine, upstream, gate_weight, up_weight, down_weight):
    block_count = TOKENS // TOK_DEV
    pick_total = TOK_DEV * TOP
    gate_wide = gate_weight.astype(jnp.float32)
    up_wide = up_weight.astype(jnp.float32)
    down_wide = down_weight.astype(jnp.float32)
    expert_ids = jnp.arange(EXPERTS, dtype=jnp.int32)

    def block_step(totals, inputs):
        block_tokens, block_routes, block_combine, block_upstream = inputs
        flat_ids = block_routes.reshape(-1).astype(jnp.int32)
        match_table = (flat_ids[:, None] == expert_ids[None, :]).astype(jnp.int32)
        position = jnp.sum((jnp.cumsum(match_table, axis=0) - 1) * match_table, axis=1)
        slot_index = (flat_ids * CAP + position).astype(jnp.int32)
        pick_index = jnp.arange(pick_total, dtype=jnp.int32)
        owners = pick_index // TOP
        token_source = jnp.full((EXPERTS * CAP,), TOK_DEV, jnp.int32).at[slot_index].set(owners)
        pick_source = jnp.full((EXPERTS * CAP,), pick_total, jnp.int32).at[slot_index].set(pick_index)
        input_rows = jnp.take(block_tokens, token_source, axis=0, mode="fill", fill_value=0)
        input_rows = input_rows.reshape(EXPERTS, CAP, D).astype(jnp.float32)
        gate_pre = jnp.einsum("ecd,edf->ecf", input_rows, gate_wide)
        up_pre = jnp.einsum("ecd,edf->ecf", input_rows, up_wide)
        hidden = narrow(jax.nn.silu(gate_pre) * up_pre).astype(jnp.float32)
        results = narrow(jnp.einsum("ecf,edf->ecd", hidden, down_wide)).astype(jnp.float32)
        pick_rows = results.reshape(EXPERTS * CAP, D)[slot_index].reshape(TOK_DEV, TOP, D)
        upstream_wide = block_upstream.astype(jnp.float32)
        layer_rows = jnp.sum(block_combine[:, :, None] * pick_rows, axis=1).astype(jnp.bfloat16)
        combine_rows = jnp.sum(upstream_wide[:, None, :] * pick_rows, axis=2)
        pick_cotangent = narrow(block_combine[:, :, None] * upstream_wide[:, None, :]).reshape(pick_total, D)
        cot_rows = jnp.take(pick_cotangent, pick_source, axis=0, mode="fill", fill_value=0)
        cot_rows = cot_rows.reshape(EXPERTS, CAP, D).astype(jnp.float32)
        hidden_grad = jnp.einsum("ecd,edf->ecf", cot_rows, down_wide)
        sigmoid_value = jax.nn.sigmoid(gate_pre)
        gate_delta = narrow(hidden_grad * up_pre * sigmoid_value * (1.0 + gate_pre * (1.0 - sigmoid_value))).astype(jnp.float32)
        up_delta = narrow(hidden_grad * jax.nn.silu(gate_pre)).astype(jnp.float32)
        input_grads = jnp.einsum("ecf,edf->ecd", gate_delta, gate_wide) + jnp.einsum("ecf,edf->ecd", up_delta, up_wide)
        input_grads = narrow(input_grads).astype(jnp.float32)
        pick_grads = input_grads.reshape(EXPERTS * CAP, D)[slot_index].reshape(TOK_DEV, TOP, D)
        token_rows = jnp.sum(pick_grads, axis=1).astype(jnp.bfloat16)
        gate_total = totals[0] + jnp.einsum("ecd,ecf->edf", input_rows, gate_delta)
        up_total = totals[1] + jnp.einsum("ecd,ecf->edf", input_rows, up_delta)
        return (gate_total, up_total), (layer_rows, token_rows, combine_rows)

    start_totals = (jnp.zeros((EXPERTS, D, F), jnp.float32), jnp.zeros((EXPERTS, D, F), jnp.float32))
    scanned = (tokens.reshape(block_count, TOK_DEV, D), routing.reshape(block_count, TOK_DEV, TOP),
               combine.reshape(block_count, TOK_DEV, TOP), upstream.reshape(block_count, TOK_DEV, D))
    totals, outputs = lax.scan(block_step, start_totals, scanned)
    layer_output = outputs[0].reshape(TOKENS, D)
    token_grad = outputs[1].reshape(TOKENS, D)
    combine_grad = outputs[2].reshape(TOKENS, TOP)
    gate_grad = totals[0] / GROUPS
    up_grad = totals[1] / GROUPS
    return (layer_output, token_grad, combine_grad, gate_grad, up_grad)
```

```python
import functools

import jax
import jax.numpy as jnp
from jax import lax
from jax.experimental import pallas as pl
from jax.experimental.pallas import tpu as pltpu
from jax.sharding import PartitionSpec as P

BF = jnp.bfloat16
F32 = jnp.float32


def dot(a, b, ca, cb):
    return lax.dot_general(a, b, (((ca,), (cb,)), ((), ())), preferred_element_type=F32)


def layer_kernel(
    E, G, cap,
    tokens, routing, combine, upstream, gate_w, up_w, down_w,
    out, token_grad, combine_grad, gate_grad, up_grad,
    gu_full, dn_full, x_send, c_send, x_arr, c_arr, y_send, d_send, y_back, d_back,
    pres, deltas, rs_send, rs_arr, rs_own,
    row_ss, row_rs, w_ss, w_rs, g_ss, g_rs,
):
    T, D = tokens.shape
    F = gate_w.shape[2]
    shard = gate_w.shape[1]
    z = lax.axis_index("expert")
    g = lax.axis_index("dp")

    barrier = pltpu.get_barrier_semaphore()

    def greet_row(k, c):
        pl.semaphore_signal(barrier, inc=1, device_id={"expert": lax.rem(z + k, E)})
        return c

    def greet_plane(k, c):
        pl.semaphore_signal(barrier, inc=1, device_id={"dp": lax.rem(g + k, G)})
        return c

    lax.fori_loop(1, E, greet_row, 0)
    lax.fori_loop(1, G, greet_plane, 0)

    mine = pl.ds(pl.multiple_of(g * shard, shard), shard)
    gu_full[mine, pl.ds(0, F)] = gate_w[0]
    gu_full[mine, pl.ds(F, F)] = up_w[0]
    dn_full[mine, :] = down_w[0]

    r = routing[...]
    e_iota = lax.broadcasted_iota(jnp.int32, (T, E), 1)
    hit = [(r[:, k : k + 1] == e_iota) for k in range(2)]
    named = (hit[0] | hit[1]).astype(F32).astype(BF)
    before = (
        lax.broadcasted_iota(jnp.int32, (T, T), 1) < lax.broadcasted_iota(jnp.int32, (T, T), 0)
    ).astype(F32).astype(BF)
    rank = dot(before, named, 1, 0)
    s_iota = lax.broadcasted_iota(jnp.int32, (T, E * cap), 1)
    place = []
    for k in range(2):
        rank_k = jnp.sum(jnp.where(hit[k], rank, 0.0), axis=1, keepdims=True)
        slot = r[:, k : k + 1] * cap + rank_k.astype(jnp.int32)
        place.append((slot == s_iota).astype(F32).astype(BF))
    x_send[...] = dot(place[0] + place[1], tokens[...], 0, 0).astype(BF).reshape(E, cap, D)

    pl.semaphore_wait(barrier, E - 1 + G - 1)

    def row_copy(kind, k, src, dst, back=False):
        peer = lax.rem(z + k, E)
        return pltpu.make_async_remote_copy(
            src_ref=src.at[peer],
            dst_ref=dst.at[z],
            send_sem=row_ss.at[kind, k],
            recv_sem=row_rs.at[kind, k],
            device_id={"expert": peer},
        )

    def row_recv(kind, k, src, dst):
        peer = lax.rem(z + k, E)
        origin = lax.rem(z + E - k, E)
        return pltpu.make_async_remote_copy(
            src_ref=src.at[peer],
            dst_ref=dst.at[origin],
            send_sem=row_ss.at[kind, k],
            recv_sem=row_rs.at[kind, k],
            device_id={"expert": peer},
        )

    def start_rows(kind, src, dst):
        def body(k, c):
            row_copy(kind, k, src, dst).start()
            return c

        lax.fori_loop(1, E, body, 0)

    def weight_copy(part, k, ref, rows):
        peer = lax.rem(g + k, G)
        return pltpu.make_async_remote_copy(
            src_ref=ref.at[mine],
            dst_ref=ref.at[rows],
            send_sem=w_ss.at[part, k],
            recv_sem=w_rs.at[part, k],
            device_id={"dp": peer},
        )

    def start_weights(k, c):
        weight_copy(0, k, gu_full, mine).start()
        weight_copy(1, k, dn_full, mine).start()
        return c

    start_rows(0, x_send, x_arr)
    lax.fori_loop(1, G, start_weights, 0)

    uw = upstream[...].astype(F32)
    cot = [(combine[:, k : k + 1] * uw).astype(BF) for k in range(2)]
    c_all = dot(jnp.concatenate(place, axis=0), jnp.concatenate(cot, axis=0), 0, 0)
    c_send[...] = c_all.astype(BF).reshape(E, cap, D)
    start_rows(1, c_send, c_arr)
    x_arr[z] = x_send[z]
    c_arr[z] = c_send[z]

    def wait_weights(k, c):
        origin = lax.rem(g + G - k, G)
        rows = pl.ds(pl.multiple_of(origin * shard, shard), shard)
        weight_copy(0, k, gu_full, rows).wait_recv()
        weight_copy(1, k, dn_full, rows).wait_recv()
        return c

    lax.fori_loop(1, G, wait_weights, 0)

    def forward(o):
        pre = dot(x_arr[o], gu_full[...], 1, 0)
        pres[o] = pre
        gp, up = pre[:, :F], pre[:, F:]
        hidden = (gp / (1.0 + jnp.exp(-gp)) * up).astype(BF)
        return dot(hidden, dn_full[...], 1, 1).astype(BF)

    def backward(o):
        hg = dot(c_arr[o], dn_full[...], 1, 0)
        pre = pres[o]
        gp, up = pre[:, :F], pre[:, F:]
        s = 1.0 / (1.0 + jnp.exp(-gp))
        rows = pl.ds(pl.multiple_of(o * cap, cap), cap)
        deltas[rows, pl.ds(0, F)] = (hg * up * s * (1.0 + gp * (1.0 - s))).astype(BF)
        deltas[rows, pl.ds(F, F)] = (hg * (gp * s)).astype(BF)
        return dot(deltas[rows, :], gu_full[...], 1, 1).astype(BF)

    def forward_step(k, c):
        o = lax.rem(z + E - k, E)

        @pl.when(k > 0)
        def _():
            row_recv(0, k, x_send, x_arr).wait_recv()

        y_send[o] = forward(o)

        @pl.when(k > 0)
        def _():
            row_copy(2, E - k, y_send, y_back).start()

        return c

    lax.fori_loop(0, E, forward_step, 0)

    def backward_step(k, c):
        o = lax.rem(z + E - k, E)

        @pl.when(k > 0)
        def _():
            row_recv(1, k, c_send, c_arr).wait_recv()

        d_send[o] = backward(o)

        @pl.when(k > 0)
        def _():
            row_copy(3, E - k, d_send, d_back).start()

        return c

    lax.fori_loop(0, E, backward_step, 0)
    y_back[z] = y_send[z]
    d_back[z] = d_send[z]

    def grad_copy(k, dst):
        peer = lax.rem(g + k, G)
        return pltpu.make_async_remote_copy(
            src_ref=rs_send.at[peer],
            dst_ref=rs_arr.at[dst],
            send_sem=g_ss.at[k],
            recv_sem=g_rs.at[k],
            device_id={"dp": peer},
        )

    if shard % 128 == 0:

        def piece(d):
            cols = pl.ds(pl.multiple_of(d * shard, shard), shard)
            return dot(x_arr[:, :, cols].reshape(E * cap, shard), deltas[...], 0, 0)

        def grad_step(k, c):
            peer = lax.rem(g + k, G)
            rs_send[peer] = piece(peer).astype(BF)
            grad_copy(k, g).start()
            return c

        lax.fori_loop(1, G, grad_step, 0)
        rs_own[...] = piece(g)
    else:
        per = 128 // shard

        def grad_chunk(c, carry):
            cols = pl.ds(pl.multiple_of(c * 128, 128), 128)
            full = dot(x_arr[:, :, cols].reshape(E * cap, 128), deltas[...], 0, 0)
            rs_send[pl.ds(c * per, per)] = full.astype(BF).reshape(per, shard, 2 * F)
            return carry

        lax.fori_loop(0, D // 128, grad_chunk, 0)

        def grad_start(k, c):
            grad_copy(k, g).start()
            return c

        lax.fori_loop(1, G, grad_start, 0)
        rs_own[...] = rs_send[g].astype(F32)

    def wait_y(k, c):
        row_recv(2, k, y_send, y_back).wait_recv()
        return c

    lax.fori_loop(1, E, wait_y, 0)
    total = jnp.zeros((T, D), F32)
    y_all = y_back[...].reshape(E * cap, D)
    u32 = upstream[...].astype(F32)
    for k in range(2):
        picked = dot(place[k], y_all, 1, 0)
        total = total + combine[:, k : k + 1] * picked
        combine_grad[:, k : k + 1] = jnp.sum(u32 * picked, axis=1, keepdims=True)
    out[...] = total.astype(BF)

    def add_piece(k, c):
        origin = lax.rem(g + G - k, G)
        grad_copy(k, origin).wait_recv()
        rs_own[...] += rs_arr[origin].astype(F32)
        return c

    lax.fori_loop(1, G, add_piece, 0)
    gate_grad[0] = rs_own[:, pl.ds(0, F)] * (1.0 / G)
    up_grad[0] = rs_own[:, pl.ds(F, F)] * (1.0 / G)

    def wait_d(k, c):
        row_recv(3, k, d_send, d_back).wait_recv()
        return c

    lax.fori_loop(1, E, wait_d, 0)
    d_all = d_back[...].reshape(E * cap, D)
    token_grad[...] = dot(place[0] + place[1], d_all, 1, 0).astype(BF)

    def end_rows(k, c):
        row_copy(0, k, x_send, x_arr).wait_send()
        row_copy(1, k, c_send, c_arr).wait_send()
        row_copy(2, k, y_send, y_back).wait_send()
        row_copy(3, k, d_send, d_back).wait_send()
        return c

    def end_plane(k, c):
        weight_copy(0, k, gu_full, mine).wait_send()
        weight_copy(1, k, dn_full, mine).wait_send()
        grad_copy(k, g).wait_send()
        return c

    lax.fori_loop(1, E, end_rows, 0)
    lax.fori_loop(1, G, end_plane, 0)


def solution(mesh):
    E = mesh.shape["expert"]
    G = mesh.shape["dp"]

    def shards(tokens, routing, combine, upstream, gate_w, up_w, down_w):
        T, D = tokens.shape
        top = routing.shape[1]
        shard, F = gate_w.shape[1:]
        cap = max(T // 2, top * T // E + T // 4)
        rows = (E, cap, D)
        vmem = pl.BlockSpec(memory_space=pltpu.VMEM)
        return pl.pallas_call(
            functools.partial(layer_kernel, E, G, cap),
            out_shape=(
                jax.ShapeDtypeStruct((T, D), BF),
                jax.ShapeDtypeStruct((T, D), BF),
                jax.ShapeDtypeStruct((T, top), F32),
                jax.ShapeDtypeStruct((1, shard, F), F32),
                jax.ShapeDtypeStruct((1, shard, F), F32),
            ),
            in_specs=[vmem] * 7,
            out_specs=(vmem,) * 5,
            scratch_shapes=[
                pltpu.VMEM((G * shard, 2 * F), BF),
                pltpu.VMEM((G * shard, F), BF),
            ]
            + [pltpu.VMEM(rows, BF)] * 8
            + [
                pltpu.VMEM((E, cap, 2 * F), F32),
                pltpu.VMEM((E * cap, 2 * F), BF),
                pltpu.VMEM((G, shard, 2 * F), BF),
                pltpu.VMEM((G, shard, 2 * F), BF),
                pltpu.VMEM((shard, 2 * F), F32),
                pltpu.SemaphoreType.DMA((4, E)),
                pltpu.SemaphoreType.DMA((4, E)),
                pltpu.SemaphoreType.DMA((2, G)),
                pltpu.SemaphoreType.DMA((2, G)),
                pltpu.SemaphoreType.DMA((G,)),
                pltpu.SemaphoreType.DMA((G,)),
            ],
            compiler_params=pltpu.CompilerParams(
                collective_id=0, has_side_effects=True, vmem_limit_bytes=52 * 2**20
            ),
            cost_estimate=pl.CostEstimate(
                flops=16 * E * cap * D * F, bytes_accessed=8 * E * cap * D * 2, transcendentals=0
            ),
        )(tokens, routing, combine, upstream, gate_w, up_w, down_w)

    rows = P(("dp", "expert"), None)
    weights = P("expert", "dp", None)
    return jax.shard_map(
        shards,
        mesh=mesh,
        in_specs=(rows, rows, rows, rows, weights, weights, weights),
        out_specs=(rows, rows, rows, weights, weights),
        check_vma=False,
    )
```

```python
import functools

import jax
import jax.numpy as jnp
from jax import lax
from jax.experimental import pallas as pl
from jax.experimental.pallas import tpu as pltpu
from jax.sharding import PartitionSpec as P

BF = jnp.bfloat16
F32 = jnp.float32


def dot(a, b, ca, cb):
    return lax.dot_general(a, b, (((ca,), (cb,)), ((), ())), preferred_element_type=F32)


def layer_kernel(
    E, G, cap,
    tokens_hbm, routing_rows, combine_rows, upstream_hbm, gate_w, up_w, down_w,
    out, token_grad, combine_grad, gate_grad, up_grad,
    tokens, upstream,
    gu_full, dn_full, x_send, c_send, x_arr, c_arr, y_send, d_send, y_back, d_back,
    pres, deltas, full_grad, mate_send, mate_arr, rs_send, rs_arr, rs_own,
    in_sem, row_ss, row_rs, w_ss, w_rs, f_ss, f_rs, m_ss, m_rs, g_ss, g_rs,
):
    T, D = tokens.shape
    C = G // 2
    F = gate_w.shape[2]
    shard = gate_w.shape[1]
    z = lax.axis_index("expert")
    g = lax.axis_index("dp")

    chip, core = lax.div(g, 2), lax.rem(g, 2)
    mate = g + 1 - 2 * core

    def twin(k):
        return lax.rem(chip + k, C) * 2 + core

    mine = pl.ds(pl.multiple_of(g * shard, shard), shard)
    loads = [
        pltpu.make_async_copy(src, dst, in_sem.at[i])
        for i, (src, dst) in enumerate(
            (
                (tokens_hbm, tokens),
                (gate_w.at[0], gu_full.at[mine, pl.ds(0, F)]),
                (up_w.at[0], gu_full.at[mine, pl.ds(F, F)]),
                (down_w.at[0], dn_full.at[mine]),
                (upstream_hbm, upstream),
            )
        )
    ]
    for load in loads:
        load.start()

    barrier = pltpu.get_barrier_semaphore()

    def greet_row(k, c):
        pl.semaphore_signal(barrier, inc=1, device_id={"expert": lax.rem(z + k, E)})
        return c

    def greet_plane(k, c):
        pl.semaphore_signal(barrier, inc=1, device_id={"dp": twin(k)})
        return c

    lax.fori_loop(1, E, greet_row, 0)
    lax.fori_loop(1, C, greet_plane, 0)
    pl.semaphore_signal(barrier, inc=1, device_id={"dp": mate})

    both = jnp.concatenate([routing_rows[...].astype(F32), combine_rows[...]] * 2, axis=0)
    columns = both.T
    r = columns[:, 0:2].astype(jnp.int32)
    combine = columns[:, 2:4]
    e_iota = lax.broadcasted_iota(jnp.int32, (T, E), 1)
    hit = [(r[:, k : k + 1] == e_iota) for k in range(2)]
    named = (hit[0] | hit[1]).astype(F32).astype(BF)
    before = (
        lax.broadcasted_iota(jnp.int32, (T, T), 1) < lax.broadcasted_iota(jnp.int32, (T, T), 0)
    ).astype(F32).astype(BF)
    rank = dot(before, named, 1, 0)
    s_iota = lax.broadcasted_iota(jnp.int32, (T, E * cap), 1)
    place = []
    for k in range(2):
        rank_k = jnp.sum(jnp.where(hit[k], rank, 0.0), axis=1, keepdims=True)
        slot = r[:, k : k + 1] * cap + rank_k.astype(jnp.int32)
        place.append((slot == s_iota).astype(F32).astype(BF))
    loads[0].wait()
    x_send[...] = dot(place[0] + place[1], tokens[...], 0, 0).astype(BF).reshape(E, cap, D)

    pl.semaphore_wait(barrier, E - 1 + C)

    def row_copy(kind, k, src, dst, back=False):
        peer = lax.rem(z + k, E)
        return pltpu.make_async_remote_copy(
            src_ref=src.at[peer],
            dst_ref=dst.at[z],
            send_sem=row_ss.at[kind, k],
            recv_sem=row_rs.at[kind, k],
            device_id={"expert": peer},
        )

    def row_recv(kind, k, src, dst):
        peer = lax.rem(z + k, E)
        origin = lax.rem(z + E - k, E)
        return pltpu.make_async_remote_copy(
            src_ref=src.at[peer],
            dst_ref=dst.at[origin],
            send_sem=row_ss.at[kind, k],
            recv_sem=row_rs.at[kind, k],
            device_id={"expert": peer},
        )

    def start_rows(kind, src, dst):
        def body(k, c):
            row_copy(kind, k, src, dst).start()
            return c

        lax.fori_loop(1, E, body, 0)

    def weight_copy(part, k, ref, rows):
        return pltpu.make_async_remote_copy(
            src_ref=ref.at[mine],
            dst_ref=ref.at[rows],
            send_sem=w_ss.at[part, k],
            recv_sem=w_rs.at[part, k],
            device_id={"dp": twin(k)},
        )

    def mate_copy(part, k, ref, rows):
        return pltpu.make_async_remote_copy(
            src_ref=ref.at[rows],
            dst_ref=ref.at[rows],
            send_sem=f_ss.at[part, k],
            recv_sem=f_rs.at[part, k],
            device_id={"dp": mate},
        )

    def rows_of(k, which):
        origin = lax.rem(chip + C - k, C) * 2 + which
        return pl.ds(pl.multiple_of(origin * shard, shard), shard)

    def start_weights(k, c):
        weight_copy(0, k, gu_full, mine).start()
        weight_copy(1, k, dn_full, mine).start()
        return c

    start_rows(0, x_send, x_arr)
    for load in loads[1:]:
        load.wait()
    lax.fori_loop(1, C, start_weights, 0)
    mate_copy(0, 0, gu_full, mine).start()
    mate_copy(1, 0, dn_full, mine).start()

    uw = upstream[...].astype(F32)
    cot = [(combine[:, k : k + 1] * uw).astype(BF) for k in range(2)]
    c_all = dot(jnp.concatenate(place, axis=0), jnp.concatenate(cot, axis=0), 0, 0)
    c_send[...] = c_all.astype(BF).reshape(E, cap, D)
    x_arr[z] = x_send[z]
    c_arr[z] = c_send[z]

    def forward_weights(k, c):
        rows = rows_of(k, core)
        weight_copy(0, k, gu_full, rows).wait_recv()
        mate_copy(0, k, gu_full, rows).start()
        weight_copy(1, k, dn_full, rows).wait_recv()
        mate_copy(1, k, dn_full, rows).start()
        return c

    lax.fori_loop(1, C, forward_weights, 0)
    start_rows(1, c_send, c_arr)

    def wait_weights(k, c):
        rows = rows_of(k, 1 - core)
        mate_copy(0, k, gu_full, rows).wait_recv()
        mate_copy(1, k, dn_full, rows).wait_recv()
        return c

    lax.fori_loop(0, C, wait_weights, 0)

    def forward(o):
        pre = dot(x_arr[o], gu_full[...], 1, 0)
        pres[o] = pre
        gp, up = pre[:, :F], pre[:, F:]
        hidden = (gp / (1.0 + jnp.exp(-gp)) * up).astype(BF)
        return dot(hidden, dn_full[...], 1, 1).astype(BF)

    def backward(o):
        hg = dot(c_arr[o], dn_full[...], 1, 0)
        pre = pres[o]
        gp, up = pre[:, :F], pre[:, F:]
        s = 1.0 / (1.0 + jnp.exp(-gp))
        rows = pl.ds(pl.multiple_of(o * cap, cap), cap)
        deltas[rows, pl.ds(0, F)] = (hg * up * s * (1.0 + gp * (1.0 - s))).astype(BF)
        deltas[rows, pl.ds(F, F)] = (hg * (gp * s)).astype(BF)
        return dot(deltas[rows, :], gu_full[...], 1, 1).astype(BF)

    def forward_step(k, c):
        o = lax.rem(z + E - k, E)

        @pl.when(k > 0)
        def _():
            row_recv(0, k, x_send, x_arr).wait_recv()

        y_send[o] = forward(o)

        @pl.when(k > 0)
        def _():
            row_copy(2, E - k, y_send, y_back).start()

        return c

    lax.fori_loop(0, E, forward_step, 0)

    def backward_step(k, c):
        o = lax.rem(z + E - k, E)

        @pl.when(k > 0)
        def _():
            row_recv(1, k, c_send, c_arr).wait_recv()

        d_send[o] = backward(o)

        @pl.when(k > 0)
        def _():
            row_copy(3, E - k, d_send, d_back).start()

        return c

    lax.fori_loop(0, E, backward_step, 0)
    y_back[z] = y_send[z]
    d_back[z] = d_send[z]

    def mate_piece(k):
        return pltpu.make_async_remote_copy(
            src_ref=mate_send.at[k],
            dst_ref=mate_arr.at[k],
            send_sem=m_ss.at[k],
            recv_sem=m_rs.at[k],
            device_id={"dp": mate},
        )

    def grad_copy(k):
        return pltpu.make_async_remote_copy(
            src_ref=rs_send.at[k],
            dst_ref=rs_arr.at[k],
            send_sem=g_ss.at[k],
            recv_sem=g_rs.at[k],
            device_id={"dp": twin(k)},
        )

    if shard % 128 == 0:

        def piece(d):
            cols = pl.ds(pl.multiple_of(d * shard, shard), shard)
            return dot(x_arr[:, :, cols].reshape(E * cap, shard), deltas[...], 0, 0)

    else:
        per = 128 // shard

        def grad_chunk(c, carry):
            cols = pl.ds(pl.multiple_of(c * 128, 128), 128)
            full = dot(x_arr[:, :, cols].reshape(E * cap, 128), deltas[...], 0, 0)
            full_grad[pl.ds(c * per, per)] = full.reshape(per, shard, 2 * F)
            return carry

        lax.fori_loop(0, D // 128, grad_chunk, 0)

        def piece(d):
            return full_grad[d]

    def mate_step(j, c):
        k = lax.rem(j + 1, C)
        mate_send[k] = piece(twin(k) + 1 - 2 * core).astype(BF)
        mate_piece(k).start()
        return c

    lax.fori_loop(0, C, mate_step, 0)

    def grad_step(k, c):
        own = piece(twin(k))
        mate_piece(k).wait_recv()
        rs_send[k] = (own + mate_arr[k].astype(F32)).astype(BF)
        grad_copy(k).start()
        return c

    lax.fori_loop(1, C, grad_step, 0)
    own = piece(g)
    mate_piece(0).wait_recv()
    rs_own[...] = own + mate_arr[0].astype(F32)

    def wait_y(k, c):
        row_recv(2, k, y_send, y_back).wait_recv()
        return c

    lax.fori_loop(1, E, wait_y, 0)
    total = jnp.zeros((T, D), F32)
    y_all = y_back[...].reshape(E * cap, D)
    u32 = upstream[...].astype(F32)
    t_iota = lax.broadcasted_iota(jnp.int32, (T, T), 1)
    sums = jnp.zeros((T, T), F32)
    for k in range(2):
        picked = dot(place[k], y_all, 1, 0)
        total = total + combine[:, k : k + 1] * picked
        sums = jnp.where(t_iota == k, jnp.sum(u32 * picked, axis=1, keepdims=True), sums)
    combine_grad[...] = sums.T[:2]
    out[...] = total.astype(BF)

    def add_piece(k, c):
        grad_copy(k).wait_recv()
        rs_own[...] += rs_arr[k].astype(F32)
        return c

    lax.fori_loop(1, C, add_piece, 0)
    gate_grad[0] = rs_own[:, pl.ds(0, F)] * (1.0 / G)
    up_grad[0] = rs_own[:, pl.ds(F, F)] * (1.0 / G)

    def wait_d(k, c):
        row_recv(3, k, d_send, d_back).wait_recv()
        return c

    lax.fori_loop(1, E, wait_d, 0)
    d_all = d_back[...].reshape(E * cap, D)
    token_grad[...] = dot(place[0] + place[1], d_all, 1, 0).astype(BF)

    def end_rows(k, c):
        row_copy(0, k, x_send, x_arr).wait_send()
        row_copy(1, k, c_send, c_arr).wait_send()
        row_copy(2, k, y_send, y_back).wait_send()
        row_copy(3, k, d_send, d_back).wait_send()
        return c

    def end_mate(k, c):
        mate_copy(0, k, gu_full, mine).wait_send()
        mate_copy(1, k, dn_full, mine).wait_send()
        mate_piece(k).wait_send()
        return c

    def end_plane(k, c):
        weight_copy(0, k, gu_full, mine).wait_send()
        weight_copy(1, k, dn_full, mine).wait_send()
        grad_copy(k).wait_send()
        return c

    lax.fori_loop(1, E, end_rows, 0)
    lax.fori_loop(0, C, end_mate, 0)
    lax.fori_loop(1, C, end_plane, 0)


def solution(mesh):
    E = mesh.shape["expert"]
    G = mesh.shape["dp"]

    def shards(tokens, routing, combine, upstream, gate_w, up_w, down_w):
        T, D = tokens.shape
        top = routing.shape[1]
        shard, F = gate_w.shape[1:]
        cap = max(T // 2, top * T // E + T // 4)
        rows = (E, cap, D)
        vmem = pl.BlockSpec(memory_space=pltpu.VMEM)
        hbm = pl.BlockSpec(memory_space=pltpu.HBM)
        results = pl.pallas_call(
            functools.partial(layer_kernel, E, G, cap),
            out_shape=(
                jax.ShapeDtypeStruct((T, D), BF),
                jax.ShapeDtypeStruct((T, D), BF),
                jax.ShapeDtypeStruct((top, T), F32),
                jax.ShapeDtypeStruct((1, shard, F), F32),
                jax.ShapeDtypeStruct((1, shard, F), F32),
            ),
            in_specs=[hbm, vmem, vmem, hbm, hbm, hbm, hbm],
            out_specs=(vmem,) * 5,
            scratch_shapes=[
                pltpu.VMEM((T, D), BF),
                pltpu.VMEM((T, D), BF),
                pltpu.VMEM((G * shard, 2 * F), BF),
                pltpu.VMEM((G * shard, F), BF),
            ]
            + [pltpu.VMEM(rows, BF)] * 8
            + [
                pltpu.VMEM((E, cap, 2 * F), F32),
                pltpu.VMEM((E * cap, 2 * F), BF),
                pltpu.VMEM((G, shard, 2 * F), F32),
            ]
            + [pltpu.VMEM((G // 2, shard, 2 * F), BF)] * 4
            + [
                pltpu.VMEM((shard, 2 * F), F32),
                pltpu.SemaphoreType.DMA((5,)),
                pltpu.SemaphoreType.DMA((4, E)),
                pltpu.SemaphoreType.DMA((4, E)),
            ]
            + [pltpu.SemaphoreType.DMA((2, G // 2))] * 4
            + [pltpu.SemaphoreType.DMA((G // 2,))] * 4,
            compiler_params=pltpu.CompilerParams(
                collective_id=0, has_side_effects=True, vmem_limit_bytes=63 * 2**20
            ),
            cost_estimate=pl.CostEstimate(
                flops=16 * E * cap * D * F, bytes_accessed=8 * E * cap * D * 2, transcendentals=0
            ),
        )(tokens, routing.T, combine.T, upstream, gate_w, up_w, down_w)
        return (results[0], results[1], results[2].T, results[3], results[4])

    rows = P(("dp", "expert"), None)
    weights = P("expert", "dp", None)
    return jax.shard_map(
        shards,
        mesh=mesh,
        in_specs=(rows, rows, rows, rows, weights, weights, weights),
        out_specs=(rows, rows, rows, weights, weights),
        check_vma=False,
    )
```

```python
import functools

import jax
import jax.numpy as jnp
from jax import lax
from jax.experimental import pallas as pl
from jax.experimental.pallas import tpu as pltpu
from jax.sharding import PartitionSpec as P

BF = jnp.bfloat16
F32 = jnp.float32


def dot(a, b, ca, cb):
    return lax.dot_general(a, b, (((ca,), (cb,)), ((), ())), preferred_element_type=F32)


def layer_kernel(
    E, G, cap,
    tokens_hbm, routing_rows, combine_rows, upstream_hbm, gate_w, up_w, down_w,
    out, token_grad, combine_grad, gate_grad, up_grad,
    tokens, upstream, info, info_arr, block_arr, relay_send,
    gu_full, dn_full, x_send, c_send, x_arr, c_arr, y_send, d_send, y_back, d_back,
    pres, deltas, full_grad, mate_send, mate_arr, rs_send, rs_arr, rs_own,
    in_sem, row_ss, row_rs, w_ss, w_rs, f_ss, f_rs, m_ss, m_rs, g_ss, g_rs,
    b_ss, b_rs, r_ss, r_rs,
):
    T, D = tokens.shape
    C = G // 2
    relayed = E == 4
    F = gate_w.shape[2]
    shard = gate_w.shape[1]
    z = lax.axis_index("expert")
    g = lax.axis_index("dp")

    chip, core = lax.div(g, 2), lax.rem(g, 2)
    mate = g + 1 - 2 * core

    def twin(k):
        return lax.rem(chip + k, C) * 2 + core

    mine = pl.ds(pl.multiple_of(g * shard, shard), shard)
    loads = [
        pltpu.make_async_copy(src, dst, in_sem.at[i])
        for i, (src, dst) in enumerate(
            (
                (tokens_hbm, tokens),
                (gate_w.at[0], gu_full.at[mine, pl.ds(0, F)]),
                (up_w.at[0], gu_full.at[mine, pl.ds(F, F)]),
                (down_w.at[0], dn_full.at[mine]),
                (upstream_hbm, upstream),
            )
        )
    ]
    for load in loads:
        load.start()

    barrier = pltpu.get_barrier_semaphore()

    def greet_row(k, c):
        pl.semaphore_signal(barrier, inc=1, device_id={"expert": lax.rem(z + k, E)})
        return c

    def greet_plane(k, c):
        pl.semaphore_signal(barrier, inc=1, device_id={"dp": twin(k)})
        return c

    lax.fori_loop(1, E, greet_row, 0)
    lax.fori_loop(1, C, greet_plane, 0)
    pl.semaphore_signal(barrier, inc=1, device_id={"dp": mate})

    both = jnp.concatenate([routing_rows[...].astype(F32), combine_rows[...]] * 2, axis=0)
    info[...] = both

    def picks_of(rows):
        columns = rows.T
        ids = columns[:, 0:2].astype(jnp.int32)
        e_iota = lax.broadcasted_iota(jnp.int32, (T, E), 1)
        hit = [(ids[:, k : k + 1] == e_iota) for k in range(2)]
        named = (hit[0] | hit[1]).astype(F32).astype(BF)
        before = (
            lax.broadcasted_iota(jnp.int32, (T, T), 1) < lax.broadcasted_iota(jnp.int32, (T, T), 0)
        ).astype(F32).astype(BF)
        rank = dot(before, named, 1, 0)
        slots = []
        for k in range(2):
            rank_k = jnp.sum(jnp.where(hit[k], rank, 0.0), axis=1, keepdims=True)
            slots.append(ids[:, k : k + 1] * cap + rank_k.astype(jnp.int32))
        return slots, columns[:, 2:4]

    def places(slots, width, first):
        s_iota = lax.broadcasted_iota(jnp.int32, (T, width), 1) + first
        return [(slot == s_iota).astype(F32).astype(BF) for slot in slots]

    slots, combine = picks_of(both)
    place = places(slots, E * cap, 0)
    loads[0].wait()
    x_send[...] = dot(place[0] + place[1], tokens[...], 0, 0).astype(BF).reshape(E, cap, D)

    pl.semaphore_wait(barrier, E - 1 + C)

    def row_copy(kind, k, src, dst, back=False):
        peer = lax.rem(z + k, E)
        return pltpu.make_async_remote_copy(
            src_ref=src.at[peer],
            dst_ref=dst.at[z],
            send_sem=row_ss.at[kind, k],
            recv_sem=row_rs.at[kind, k],
            device_id={"expert": peer},
        )

    def row_recv(kind, k, src, dst):
        peer = lax.rem(z + k, E)
        origin = lax.rem(z + E - k, E)
        return pltpu.make_async_remote_copy(
            src_ref=src.at[peer],
            dst_ref=dst.at[origin],
            send_sem=row_ss.at[kind, k],
            recv_sem=row_rs.at[kind, k],
            device_id={"expert": peer},
        )

    def start_rows(kind, src, dst):
        def body(k, c):
            row_copy(kind, k, src, dst).start()
            return c

        lax.fori_loop(1, E, body, 0)

    def weight_copy(part, k, ref, rows):
        return pltpu.make_async_remote_copy(
            src_ref=ref.at[mine],
            dst_ref=ref.at[rows],
            send_sem=w_ss.at[part, k],
            recv_sem=w_rs.at[part, k],
            device_id={"dp": twin(k)},
        )

    def mate_copy(part, k, ref, rows):
        return pltpu.make_async_remote_copy(
            src_ref=ref.at[rows],
            dst_ref=ref.at[rows],
            send_sem=f_ss.at[part, k],
            recv_sem=f_rs.at[part, k],
            device_id={"dp": mate},
        )

    def rows_of(k, which):
        origin = lax.rem(chip + C - k, C) * 2 + which
        return pl.ds(pl.multiple_of(origin * shard, shard), shard)

    def start_weights(k, c):
        weight_copy(0, k, gu_full, mine).start()
        weight_copy(1, k, dn_full, mine).start()
        return c

    half = lax.div(z, 2)
    near = 2 - half
    partner = z + 1 - 2 * lax.rem(z, 2)
    boundary = (z == 1) | (z == 2)

    def info_copy(k, slot):
        return pltpu.make_async_remote_copy(
            src_ref=info,
            dst_ref=info_arr.at[slot],
            send_sem=row_ss.at[4, k],
            recv_sem=row_rs.at[4, k],
            device_id={"expert": lax.rem(z + k, E)},
        )

    def block_copy(kind, src, i):
        return pltpu.make_async_remote_copy(
            src_ref=src,
            dst_ref=block_arr.at[kind, i],
            send_sem=b_ss.at[kind],
            recv_sem=b_rs.at[kind, i],
            device_id={"expert": near},
        )

    def partner_copy(kind, src, dst, slot):
        return pltpu.make_async_remote_copy(
            src_ref=src.at[partner],
            dst_ref=dst.at[slot],
            send_sem=row_ss.at[kind, 1],
            recv_sem=row_rs.at[kind, 1],
            device_id={"expert": partner},
        )

    def relay_copy(kind, i, dst):
        return pltpu.make_async_remote_copy(
            src_ref=relay_send.at[kind, i],
            dst_ref=dst.at[2 * (1 - half) + i],
            send_sem=r_ss.at[kind, i],
            recv_sem=r_rs.at[kind, i],
            device_id={"expert": partner},
        )

    def near_first(j):
        return half * (1 - j) + (1 - half) * j

    def relay(kind, dst):
        @pl.when(boundary)
        def _():
            def body(j, c):
                i = near_first(j)
                o = 2 * (1 - half) + i
                block_copy(kind, tokens, i).wait_recv()
                slots_o, combine_o = picks_of(info_arr[o])
                block = block_arr[kind, i]
                if kind == 1:
                    wide = block.astype(F32)
                    block = jnp.concatenate(
                        [(combine_o[:, k : k + 1] * wide).astype(BF) for k in range(2)], axis=0
                    )

                def chosen(e):
                    found = places(slots_o, cap, e * cap)
                    found = found[0] + found[1] if kind == 0 else jnp.concatenate(found, axis=0)
                    return dot(found, block, 0, 0).astype(BF)

                relay_send[kind, i] = chosen(partner)
                relay_copy(kind, i, dst).start()
                dst[o] = chosen(z)
                return c

            lax.fori_loop(0, 2, body, 0)

    def start_info(k, c):
        info_copy(k, z).start()
        return c

    def wait_info(k, c):
        info_copy(k, lax.rem(z + E - k, E)).wait_recv()
        return c

    if relayed:
        lax.fori_loop(1, E, start_info, 0)
        block_copy(0, tokens, lax.rem(z, 2)).start()
        partner_copy(0, x_send, x_arr, z).start()
    else:
        start_rows(0, x_send, x_arr)
    for load in loads[1:]:
        load.wait()
    lax.fori_loop(1, C, start_weights, 0)
    mate_copy(0, 0, gu_full, mine).start()
    mate_copy(1, 0, dn_full, mine).start()

    uw = upstream[...].astype(F32)
    cot = [(combine[:, k : k + 1] * uw).astype(BF) for k in range(2)]
    c_all = dot(jnp.concatenate(place, axis=0), jnp.concatenate(cot, axis=0), 0, 0)
    c_send[...] = c_all.astype(BF).reshape(E, cap, D)
    x_arr[z] = x_send[z]
    c_arr[z] = c_send[z]

    def forward_weights(k, c):
        rows = rows_of(k, core)
        weight_copy(0, k, gu_full, rows).wait_recv()
        mate_copy(0, k, gu_full, rows).start()
        weight_copy(1, k, dn_full, rows).wait_recv()
        mate_copy(1, k, dn_full, rows).start()
        return c

    lax.fori_loop(1, C, forward_weights, 0)
    if relayed:
        block_copy(1, upstream, lax.rem(z, 2)).start()
        partner_copy(1, c_send, c_arr, z).start()
        lax.fori_loop(1, E, wait_info, 0)
        relay(0, x_arr)
    else:
        start_rows(1, c_send, c_arr)

    def wait_weights(k, c):
        rows = rows_of(k, 1 - core)
        mate_copy(0, k, gu_full, rows).wait_recv()
        mate_copy(1, k, dn_full, rows).wait_recv()
        return c

    lax.fori_loop(0, C, wait_weights, 0)

    def forward(o):
        pre = dot(x_arr[o], gu_full[...], 1, 0)
        pres[o] = pre
        gp, up = pre[:, :F], pre[:, F:]
        hidden = (gp / (1.0 + jnp.exp(-gp)) * up).astype(BF)
        return dot(hidden, dn_full[...], 1, 1).astype(BF)

    def backward(o):
        hg = dot(c_arr[o], dn_full[...], 1, 0)
        pre = pres[o]
        gp, up = pre[:, :F], pre[:, F:]
        s = 1.0 / (1.0 + jnp.exp(-gp))
        rows = pl.ds(pl.multiple_of(o * cap, cap), cap)
        deltas[rows, pl.ds(0, F)] = (hg * up * s * (1.0 + gp * (1.0 - s))).astype(BF)
        deltas[rows, pl.ds(F, F)] = (hg * (gp * s)).astype(BF)
        return dot(deltas[rows, :], gu_full[...], 1, 1).astype(BF)

    def origin_of(k):
        if not relayed:
            return lax.rem(z + E - k, E)
        other = 2 * (1 - half) + near_first(lax.rem(k, 2))
        return jnp.where(k == 0, z, jnp.where(k == 1, partner, other))

    def step(kind, k, src, dst, work, sent, back):
        o = origin_of(k)
        if relayed:

            @pl.when(k == 1)
            def _():
                partner_copy(kind, src, dst, partner).wait_recv()

            @pl.when((k > 1) & jnp.logical_not(boundary))
            def _():
                relay_copy(kind, near_first(lax.rem(k, 2)), dst).wait_recv()

        else:

            @pl.when(k > 0)
            def _():
                row_recv(kind, k, src, dst).wait_recv()

        sent[o] = work(o)

        @pl.when(k > 0)
        def _():
            row_copy(kind + 2, lax.rem(o - z + E, E), sent, back).start()

    def forward_step(k, c):
        step(0, k, x_send, x_arr, forward, y_send, y_back)
        return c

    def backward_step(k, c):
        step(1, k, c_send, c_arr, backward, d_send, d_back)
        return c

    if relayed:
        lax.fori_loop(0, 2, forward_step, 0)
        relay(1, c_arr)
        lax.fori_loop(2, E, forward_step, 0)
    else:
        lax.fori_loop(0, E, forward_step, 0)
    lax.fori_loop(0, E, backward_step, 0)
    y_back[z] = y_send[z]
    d_back[z] = d_send[z]

    def mate_piece(k):
        return pltpu.make_async_remote_copy(
            src_ref=mate_send.at[k],
            dst_ref=mate_arr.at[k],
            send_sem=m_ss.at[k],
            recv_sem=m_rs.at[k],
            device_id={"dp": mate},
        )

    def grad_copy(k):
        return pltpu.make_async_remote_copy(
            src_ref=rs_send.at[k],
            dst_ref=rs_arr.at[k],
            send_sem=g_ss.at[k],
            recv_sem=g_rs.at[k],
            device_id={"dp": twin(k)},
        )

    if shard % 128 == 0:

        def piece(d):
            cols = pl.ds(pl.multiple_of(d * shard, shard), shard)
            return dot(x_arr[:, :, cols].reshape(E * cap, shard), deltas[...], 0, 0)

    else:
        per = 128 // shard

        def grad_chunk(c, carry):
            cols = pl.ds(pl.multiple_of(c * 128, 128), 128)
            full = dot(x_arr[:, :, cols].reshape(E * cap, 128), deltas[...], 0, 0)
            full_grad[pl.ds(c * per, per)] = full.reshape(per, shard, 2 * F)
            return carry

        lax.fori_loop(0, D // 128, grad_chunk, 0)

        def piece(d):
            return full_grad[d]

    def mate_step(j, c):
        k = lax.rem(j + 1, C)
        mate_send[k] = piece(twin(k) + 1 - 2 * core).astype(BF)
        mate_piece(k).start()
        return c

    lax.fori_loop(0, C, mate_step, 0)

    def grad_step(k, c):
        own = piece(twin(k))
        mate_piece(k).wait_recv()
        rs_send[k] = (own + mate_arr[k].astype(F32)).astype(BF)
        grad_copy(k).start()
        return c

    lax.fori_loop(1, C, grad_step, 0)
    own = piece(g)
    mate_piece(0).wait_recv()
    rs_own[...] = own + mate_arr[0].astype(F32)

    def wait_y(k, c):
        row_recv(2, k, y_send, y_back).wait_recv()
        return c

    lax.fori_loop(1, E, wait_y, 0)
    total = jnp.zeros((T, D), F32)
    y_all = y_back[...].reshape(E * cap, D)
    u32 = upstream[...].astype(F32)
    t_iota = lax.broadcasted_iota(jnp.int32, (T, T), 1)
    sums = jnp.zeros((T, T), F32)
    for k in range(2):
        picked = dot(place[k], y_all, 1, 0)
        total = total + combine[:, k : k + 1] * picked
        sums = jnp.where(t_iota == k, jnp.sum(u32 * picked, axis=1, keepdims=True), sums)
    combine_grad[...] = sums.T[:2]
    out[...] = total.astype(BF)

    def add_piece(k, c):
        grad_copy(k).wait_recv()
        rs_own[...] += rs_arr[k].astype(F32)
        return c

    lax.fori_loop(1, C, add_piece, 0)
    gate_grad[0] = rs_own[:, pl.ds(0, F)] * (1.0 / G)
    up_grad[0] = rs_own[:, pl.ds(F, F)] * (1.0 / G)

    def wait_d(k, c):
        row_recv(3, k, d_send, d_back).wait_recv()
        return c

    lax.fori_loop(1, E, wait_d, 0)
    d_all = d_back[...].reshape(E * cap, D)
    token_grad[...] = dot(place[0] + place[1], d_all, 1, 0).astype(BF)

    def end_rows(k, c):
        if relayed:
            info_copy(k, z).wait_send()
        else:
            row_copy(0, k, x_send, x_arr).wait_send()
            row_copy(1, k, c_send, c_arr).wait_send()
        row_copy(2, k, y_send, y_back).wait_send()
        row_copy(3, k, d_send, d_back).wait_send()
        return c

    def end_mate(k, c):
        mate_copy(0, k, gu_full, mine).wait_send()
        mate_copy(1, k, dn_full, mine).wait_send()
        mate_piece(k).wait_send()
        return c

    def end_plane(k, c):
        weight_copy(0, k, gu_full, mine).wait_send()
        weight_copy(1, k, dn_full, mine).wait_send()
        grad_copy(k).wait_send()
        return c

    lax.fori_loop(1, E, end_rows, 0)
    if relayed:
        for kind, block, rows, dst in ((0, tokens, x_send, x_arr), (1, upstream, c_send, c_arr)):
            block_copy(kind, block, 0).wait_send()
            partner_copy(kind, rows, dst, z).wait_send()

            @pl.when(boundary)
            def _():
                relay_copy(kind, 0, dst).wait_send()
                relay_copy(kind, 1, dst).wait_send()

    lax.fori_loop(0, C, end_mate, 0)
    lax.fori_loop(1, C, end_plane, 0)


def solution(mesh):
    E = mesh.shape["expert"]
    G = mesh.shape["dp"]

    def shards(tokens, routing, combine, upstream, gate_w, up_w, down_w):
        T, D = tokens.shape
        top = routing.shape[1]
        shard, F = gate_w.shape[1:]
        cap = max(T // 2, top * T // E + T // 4)
        rows = (E, cap, D)
        vmem = pl.BlockSpec(memory_space=pltpu.VMEM)
        hbm = pl.BlockSpec(memory_space=pltpu.HBM)
        results = pl.pallas_call(
            functools.partial(layer_kernel, E, G, cap),
            out_shape=(
                jax.ShapeDtypeStruct((T, D), BF),
                jax.ShapeDtypeStruct((T, D), BF),
                jax.ShapeDtypeStruct((top, T), F32),
                jax.ShapeDtypeStruct((1, shard, F), F32),
                jax.ShapeDtypeStruct((1, shard, F), F32),
            ),
            in_specs=[hbm, vmem, vmem, hbm, hbm, hbm, hbm],
            out_specs=(vmem,) * 5,
            scratch_shapes=[
                pltpu.VMEM((T, D), BF),
                pltpu.VMEM((T, D), BF),
                pltpu.VMEM((4 * top, T), F32),
                pltpu.VMEM((E, 4 * top, T), F32),
                pltpu.VMEM((2, 2, T, D), BF),
                pltpu.VMEM((2, 2, cap, D), BF),
                pltpu.VMEM((G * shard, 2 * F), BF),
                pltpu.VMEM((G * shard, F), BF),
            ]
            + [pltpu.VMEM(rows, BF)] * 8
            + [
                pltpu.VMEM((E, cap, 2 * F), F32),
                pltpu.VMEM((E * cap, 2 * F), BF),
                pltpu.VMEM((G, shard, 2 * F), F32),
            ]
            + [pltpu.VMEM((G // 2, shard, 2 * F), BF)] * 4
            + [
                pltpu.VMEM((shard, 2 * F), F32),
                pltpu.SemaphoreType.DMA((5,)),
                pltpu.SemaphoreType.DMA((5, E)),
                pltpu.SemaphoreType.DMA((5, E)),
            ]
            + [pltpu.SemaphoreType.DMA((2, G // 2))] * 4
            + [pltpu.SemaphoreType.DMA((G // 2,))] * 4
            + [pltpu.SemaphoreType.DMA((2,))]
            + [pltpu.SemaphoreType.DMA((2, 2))] * 3,
            compiler_params=pltpu.CompilerParams(
                collective_id=0, has_side_effects=True, vmem_limit_bytes=63 * 2**20
            ),
            cost_estimate=pl.CostEstimate(
                flops=16 * E * cap * D * F, bytes_accessed=8 * E * cap * D * 2, transcendentals=0
            ),
        )(tokens, routing.T, combine.T, upstream, gate_w, up_w, down_w)
        return (results[0], results[1], results[2].T, results[3], results[4])

    rows = P(("dp", "expert"), None)
    weights = P("expert", "dp", None)
    return jax.shard_map(
        shards,
        mesh=mesh,
        in_specs=(rows, rows, rows, rows, weights, weights, weights),
        out_specs=(rows, rows, rows, weights, weights),
        check_vma=False,
    )
```

```python
import functools

import jax
import jax.numpy as jnp
from jax import lax
from jax.experimental import pallas as pl
from jax.experimental.pallas import tpu as pltpu
from jax.sharding import PartitionSpec as P

BF = jnp.bfloat16
F32 = jnp.float32


def dot(a, b, ca, cb):
    return lax.dot_general(a, b, (((ca,), (cb,)), ((), ())), preferred_element_type=F32)


def layer_kernel(
    E, G, cap,
    tokens_hbm, routing_rows, combine_rows, upstream_hbm, gate_w, up_w, down_w,
    out, token_grad, combine_grad, gate_grad, up_grad,
    tokens, upstream, info, info_arr, block_arr, relay_send, end_back, part_send, part_arr,
    gu_full, dn_full, x_send, c_send, x_arr, c_arr, y_send, d_send, y_back, d_back,
    pres, deltas, full_grad, mate_send, mate_arr, rs_send, rs_arr, rs_own,
    in_sem, row_ss, row_rs, w_ss, w_rs, f_ss, f_rs, m_ss, m_rs, g_ss, g_rs,
    b_ss, b_rs, r_ss, r_rs, e_ss, e_rs, p_ss, p_rs,
):
    T, D = tokens.shape
    C = G // 2
    relayed = E == 4
    F = gate_w.shape[2]
    shard = gate_w.shape[1]
    z = lax.axis_index("expert")
    g = lax.axis_index("dp")

    chip, core = lax.div(g, 2), lax.rem(g, 2)
    mate = g + 1 - 2 * core

    def twin(k):
        return lax.rem(chip + k, C) * 2 + core

    mine = pl.ds(pl.multiple_of(g * shard, shard), shard)
    loads = [
        pltpu.make_async_copy(src, dst, in_sem.at[i])
        for i, (src, dst) in enumerate(
            (
                (tokens_hbm, tokens),
                (gate_w.at[0], gu_full.at[mine, pl.ds(0, F)]),
                (up_w.at[0], gu_full.at[mine, pl.ds(F, F)]),
                (down_w.at[0], dn_full.at[mine]),
                (upstream_hbm, upstream),
            )
        )
    ]
    for load in loads:
        load.start()

    barrier = pltpu.get_barrier_semaphore()

    def greet_row(k, c):
        pl.semaphore_signal(barrier, inc=1, device_id={"expert": lax.rem(z + k, E)})
        return c

    def greet_plane(k, c):
        pl.semaphore_signal(barrier, inc=1, device_id={"dp": twin(k)})
        return c

    lax.fori_loop(1, E, greet_row, 0)
    lax.fori_loop(1, C, greet_plane, 0)
    pl.semaphore_signal(barrier, inc=1, device_id={"dp": mate})

    both = jnp.concatenate([routing_rows[...].astype(F32), combine_rows[...]] * 2, axis=0)
    info[...] = both

    def picks_of(rows):
        columns = rows.T
        ids = columns[:, 0:2].astype(jnp.int32)
        e_iota = lax.broadcasted_iota(jnp.int32, (T, E), 1)
        hit = [(ids[:, k : k + 1] == e_iota) for k in range(2)]
        named = (hit[0] | hit[1]).astype(F32).astype(BF)
        before = (
            lax.broadcasted_iota(jnp.int32, (T, T), 1) < lax.broadcasted_iota(jnp.int32, (T, T), 0)
        ).astype(F32).astype(BF)
        rank = dot(before, named, 1, 0)
        slots = []
        for k in range(2):
            rank_k = jnp.sum(jnp.where(hit[k], rank, 0.0), axis=1, keepdims=True)
            slots.append(ids[:, k : k + 1] * cap + rank_k.astype(jnp.int32))
        return slots, columns[:, 2:4]

    def places(slots, width, first):
        s_iota = lax.broadcasted_iota(jnp.int32, (T, width), 1) + first
        return [(slot == s_iota).astype(F32).astype(BF) for slot in slots]

    slots, combine = picks_of(both)
    place = places(slots, E * cap, 0)
    loads[0].wait()
    x_send[...] = dot(place[0] + place[1], tokens[...], 0, 0).astype(BF).reshape(E, cap, D)

    pl.semaphore_wait(barrier, E - 1 + C)

    def row_copy(kind, k, src, dst, back=False):
        peer = lax.rem(z + k, E)
        return pltpu.make_async_remote_copy(
            src_ref=src.at[peer],
            dst_ref=dst.at[z],
            send_sem=row_ss.at[kind, k],
            recv_sem=row_rs.at[kind, k],
            device_id={"expert": peer},
        )

    def row_recv(kind, k, src, dst):
        peer = lax.rem(z + k, E)
        origin = lax.rem(z + E - k, E)
        return pltpu.make_async_remote_copy(
            src_ref=src.at[peer],
            dst_ref=dst.at[origin],
            send_sem=row_ss.at[kind, k],
            recv_sem=row_rs.at[kind, k],
            device_id={"expert": peer},
        )

    def start_rows(kind, src, dst):
        def body(k, c):
            row_copy(kind, k, src, dst).start()
            return c

        lax.fori_loop(1, E, body, 0)

    def weight_copy(part, k, ref, rows):
        return pltpu.make_async_remote_copy(
            src_ref=ref.at[mine],
            dst_ref=ref.at[rows],
            send_sem=w_ss.at[part, k],
            recv_sem=w_rs.at[part, k],
            device_id={"dp": twin(k)},
        )

    def mate_copy(part, k, ref, rows):
        return pltpu.make_async_remote_copy(
            src_ref=ref.at[rows],
            dst_ref=ref.at[rows],
            send_sem=f_ss.at[part, k],
            recv_sem=f_rs.at[part, k],
            device_id={"dp": mate},
        )

    def rows_of(k, which):
        origin = lax.rem(chip + C - k, C) * 2 + which
        return pl.ds(pl.multiple_of(origin * shard, shard), shard)

    def start_weights(k, c):
        weight_copy(0, k, gu_full, mine).start()
        weight_copy(1, k, dn_full, mine).start()
        return c

    half = lax.div(z, 2)
    near = 2 - half
    partner = z + 1 - 2 * lax.rem(z, 2)
    boundary = (z == 1) | (z == 2)

    def info_copy(k, slot):
        return pltpu.make_async_remote_copy(
            src_ref=info,
            dst_ref=info_arr.at[slot],
            send_sem=row_ss.at[4, k],
            recv_sem=row_rs.at[4, k],
            device_id={"expert": lax.rem(z + k, E)},
        )

    def block_copy(kind, src, i):
        return pltpu.make_async_remote_copy(
            src_ref=src,
            dst_ref=block_arr.at[kind, i],
            send_sem=b_ss.at[kind],
            recv_sem=b_rs.at[kind, i],
            device_id={"expert": near},
        )

    def partner_copy(kind, src, dst, slot):
        return pltpu.make_async_remote_copy(
            src_ref=src.at[partner],
            dst_ref=dst.at[slot],
            send_sem=row_ss.at[kind, 1],
            recv_sem=row_rs.at[kind, 1],
            device_id={"expert": partner},
        )

    def relay_copy(kind, i, dst):
        return pltpu.make_async_remote_copy(
            src_ref=relay_send.at[kind, i],
            dst_ref=dst.at[2 * (1 - half) + i],
            send_sem=r_ss.at[kind, i],
            recv_sem=r_rs.at[kind, i],
            device_id={"expert": partner},
        )

    def end_copy(i):
        return pltpu.make_async_remote_copy(
            src_ref=d_send.at[2 * (1 - half) + i],
            dst_ref=end_back.at[i],
            send_sem=e_ss.at[i],
            recv_sem=e_rs.at[i],
            device_id={"expert": partner},
        )

    def part_copy(i):
        return pltpu.make_async_remote_copy(
            src_ref=part_send.at[i],
            dst_ref=part_arr,
            send_sem=p_ss.at[i],
            recv_sem=p_rs.at[0],
            device_id={"expert": 2 * (1 - half) + i},
        )

    def near_first(j):
        return half * (1 - j) + (1 - half) * j

    def relay(kind, dst):
        @pl.when(boundary)
        def _():
            def body(j, c):
                i = near_first(j)
                o = 2 * (1 - half) + i
                block_copy(kind, tokens, i).wait_recv()
                slots_o, combine_o = picks_of(info_arr[o])
                block = block_arr[kind, i]
                if kind == 1:
                    wide = block.astype(F32)
                    block = jnp.concatenate(
                        [(combine_o[:, k : k + 1] * wide).astype(BF) for k in range(2)], axis=0
                    )

                def chosen(e):
                    found = places(slots_o, cap, e * cap)
                    found = found[0] + found[1] if kind == 0 else jnp.concatenate(found, axis=0)
                    return dot(found, block, 0, 0).astype(BF)

                relay_send[kind, i] = chosen(partner)
                relay_copy(kind, i, dst).start()
                dst[o] = chosen(z)
                return c

            lax.fori_loop(0, 2, body, 0)

    def start_info(k, c):
        info_copy(k, z).start()
        return c

    def wait_info(k, c):
        info_copy(k, lax.rem(z + E - k, E)).wait_recv()
        return c

    if relayed:
        lax.fori_loop(1, E, start_info, 0)
        block_copy(0, tokens, lax.rem(z, 2)).start()
        partner_copy(0, x_send, x_arr, z).start()
    else:
        start_rows(0, x_send, x_arr)
    for load in loads[1:]:
        load.wait()
    lax.fori_loop(1, C, start_weights, 0)
    mate_copy(0, 0, gu_full, mine).start()
    mate_copy(1, 0, dn_full, mine).start()

    uw = upstream[...].astype(F32)
    cot = [(combine[:, k : k + 1] * uw).astype(BF) for k in range(2)]
    c_all = dot(jnp.concatenate(place, axis=0), jnp.concatenate(cot, axis=0), 0, 0)
    c_send[...] = c_all.astype(BF).reshape(E, cap, D)
    x_arr[z] = x_send[z]
    c_arr[z] = c_send[z]

    def forward_weights(k, c):
        rows = rows_of(k, core)
        weight_copy(0, k, gu_full, rows).wait_recv()
        mate_copy(0, k, gu_full, rows).start()
        weight_copy(1, k, dn_full, rows).wait_recv()
        mate_copy(1, k, dn_full, rows).start()
        return c

    lax.fori_loop(1, C, forward_weights, 0)
    if relayed:
        block_copy(1, upstream, lax.rem(z, 2)).start()
        partner_copy(1, c_send, c_arr, z).start()
        lax.fori_loop(1, E, wait_info, 0)
        relay(0, x_arr)
    else:
        start_rows(1, c_send, c_arr)

    def wait_weights(k, c):
        rows = rows_of(k, 1 - core)
        mate_copy(0, k, gu_full, rows).wait_recv()
        mate_copy(1, k, dn_full, rows).wait_recv()
        return c

    lax.fori_loop(0, C, wait_weights, 0)

    def forward(o):
        pre = dot(x_arr[o], gu_full[...], 1, 0)
        pres[o] = pre
        gp, up = pre[:, :F], pre[:, F:]
        hidden = (gp / (1.0 + jnp.exp(-gp)) * up).astype(BF)
        return dot(hidden, dn_full[...], 1, 1).astype(BF)

    def backward(o):
        hg = dot(c_arr[o], dn_full[...], 1, 0)
        pre = pres[o]
        gp, up = pre[:, :F], pre[:, F:]
        s = 1.0 / (1.0 + jnp.exp(-gp))
        rows = pl.ds(pl.multiple_of(o * cap, cap), cap)
        deltas[rows, pl.ds(0, F)] = (hg * up * s * (1.0 + gp * (1.0 - s))).astype(BF)
        deltas[rows, pl.ds(F, F)] = (hg * (gp * s)).astype(BF)
        return dot(deltas[rows, :], gu_full[...], 1, 1).astype(BF)

    def origin_of(k):
        if not relayed:
            return lax.rem(z + E - k, E)
        other = 2 * (1 - half) + near_first(lax.rem(k, 2))
        return jnp.where(k == 0, z, jnp.where(k == 1, partner, other))

    def step(kind, k, src, dst, work, sent, back):
        o = origin_of(k)
        if relayed:

            @pl.when(k == 1)
            def _():
                partner_copy(kind, src, dst, partner).wait_recv()

            @pl.when((k > 1) & jnp.logical_not(boundary))
            def _():
                relay_copy(kind, near_first(lax.rem(k, 2)), dst).wait_recv()

        else:

            @pl.when(k > 0)
            def _():
                row_recv(kind, k, src, dst).wait_recv()

        sent[o] = work(o)

        summed = relayed and kind == 1

        @pl.when((k == 1) if summed else (k > 0))
        def _():
            row_copy(kind + 2, lax.rem(o - z + E, E), sent, back).start()

        if summed:

            @pl.when((k > 1) & jnp.logical_not(boundary))
            def _():
                end_copy(near_first(lax.rem(k, 2))).start()

    def forward_step(k, c):
        step(0, k, x_send, x_arr, forward, y_send, y_back)
        return c

    def backward_step(k, c):
        step(1, k, c_send, c_arr, backward, d_send, d_back)
        return c

    if relayed:
        lax.fori_loop(0, 2, forward_step, 0)
        relay(1, c_arr)
        lax.fori_loop(2, E, forward_step, 0)
    else:
        lax.fori_loop(0, E, forward_step, 0)
    lax.fori_loop(0, E, backward_step, 0)

    if relayed:
        d_back[2 * (1 - half)] = jnp.zeros((cap, D), BF)
        d_back[2 * (1 - half) + 1] = jnp.zeros((cap, D), BF)

        @pl.when(boundary)
        def _():
            def body(j, c):
                i = near_first(j)
                o = 2 * (1 - half) + i
                slots_o, _ = picks_of(info_arr[o])
                found = places(slots_o, cap, z * cap)
                sums = dot(found[0] + found[1], d_send[o], 1, 0)
                found = places(slots_o, cap, partner * cap)
                end_copy(i).wait_recv()
                sums = sums + dot(found[0] + found[1], end_back[i], 1, 0)
                part_send[i] = sums.astype(BF)
                part_copy(i).start()
                return c

            lax.fori_loop(0, 2, body, 0)

    y_back[z] = y_send[z]
    d_back[z] = d_send[z]

    def mate_piece(k):
        return pltpu.make_async_remote_copy(
            src_ref=mate_send.at[k],
            dst_ref=mate_arr.at[k],
            send_sem=m_ss.at[k],
            recv_sem=m_rs.at[k],
            device_id={"dp": mate},
        )

    def grad_copy(k):
        return pltpu.make_async_remote_copy(
            src_ref=rs_send.at[k],
            dst_ref=rs_arr.at[k],
            send_sem=g_ss.at[k],
            recv_sem=g_rs.at[k],
            device_id={"dp": twin(k)},
        )

    if shard % 128 == 0:

        def piece(d):
            cols = pl.ds(pl.multiple_of(d * shard, shard), shard)
            return dot(x_arr[:, :, cols].reshape(E * cap, shard), deltas[...], 0, 0)

    else:
        per = 128 // shard

        def grad_chunk(c, carry):
            cols = pl.ds(pl.multiple_of(c * 128, 128), 128)
            full = dot(x_arr[:, :, cols].reshape(E * cap, 128), deltas[...], 0, 0)
            full_grad[pl.ds(c * per, per)] = full.reshape(per, shard, 2 * F)
            return carry

        lax.fori_loop(0, D // 128, grad_chunk, 0)

        def piece(d):
            return full_grad[d]

    def mate_step(j, c):
        k = lax.rem(j + 1, C)
        mate_send[k] = piece(twin(k) + 1 - 2 * core).astype(BF)
        mate_piece(k).start()
        return c

    lax.fori_loop(0, C, mate_step, 0)

    def grad_step(k, c):
        own = piece(twin(k))
        mate_piece(k).wait_recv()
        rs_send[k] = (own + mate_arr[k].astype(F32)).astype(BF)
        grad_copy(k).start()
        return c

    lax.fori_loop(1, C, grad_step, 0)
    own = piece(g)
    mate_piece(0).wait_recv()
    rs_own[...] = own + mate_arr[0].astype(F32)

    def wait_y(k, c):
        row_recv(2, k, y_send, y_back).wait_recv()
        return c

    lax.fori_loop(1, E, wait_y, 0)
    total = jnp.zeros((T, D), F32)
    y_all = y_back[...].reshape(E * cap, D)
    u32 = upstream[...].astype(F32)
    t_iota = lax.broadcasted_iota(jnp.int32, (T, T), 1)
    sums = jnp.zeros((T, T), F32)
    for k in range(2):
        picked = dot(place[k], y_all, 1, 0)
        total = total + combine[:, k : k + 1] * picked
        sums = jnp.where(t_iota == k, jnp.sum(u32 * picked, axis=1, keepdims=True), sums)
    combine_grad[...] = sums.T[:2]
    out[...] = total.astype(BF)

    def add_piece(k, c):
        grad_copy(k).wait_recv()
        rs_own[...] += rs_arr[k].astype(F32)
        return c

    lax.fori_loop(1, C, add_piece, 0)
    gate_grad[0] = rs_own[:, pl.ds(0, F)] * (1.0 / G)
    up_grad[0] = rs_own[:, pl.ds(F, F)] * (1.0 / G)

    def wait_d(k, c):
        row_recv(3, k, d_send, d_back).wait_recv()
        return c

    if relayed:
        wait_d(lax.rem(z - partner + E, E), 0)
        part_copy(0).wait_recv()
    else:
        lax.fori_loop(1, E, wait_d, 0)
    d_all = d_back[...].reshape(E * cap, D)
    sums = dot(place[0] + place[1], d_all, 1, 0)
    if relayed:
        sums = sums + part_arr[...].astype(F32)
    token_grad[...] = sums.astype(BF)

    def end_rows(k, c):
        if relayed:
            info_copy(k, z).wait_send()
        else:
            row_copy(0, k, x_send, x_arr).wait_send()
            row_copy(1, k, c_send, c_arr).wait_send()
        row_copy(2, k, y_send, y_back).wait_send()
        if not relayed:
            row_copy(3, k, d_send, d_back).wait_send()
        return c

    def end_mate(k, c):
        mate_copy(0, k, gu_full, mine).wait_send()
        mate_copy(1, k, dn_full, mine).wait_send()
        mate_piece(k).wait_send()
        return c

    def end_plane(k, c):
        weight_copy(0, k, gu_full, mine).wait_send()
        weight_copy(1, k, dn_full, mine).wait_send()
        grad_copy(k).wait_send()
        return c

    lax.fori_loop(1, E, end_rows, 0)
    if relayed:
        row_copy(3, lax.rem(partner - z + E, E), d_send, d_back).wait_send()

        @pl.when(boundary)
        def _():
            part_copy(0).wait_send()
            part_copy(1).wait_send()

        @pl.when(jnp.logical_not(boundary))
        def _():
            end_copy(0).wait_send()
            end_copy(1).wait_send()

        for kind, block, rows, dst in ((0, tokens, x_send, x_arr), (1, upstream, c_send, c_arr)):
            block_copy(kind, block, 0).wait_send()
            partner_copy(kind, rows, dst, z).wait_send()

            @pl.when(boundary)
            def _():
                relay_copy(kind, 0, dst).wait_send()
                relay_copy(kind, 1, dst).wait_send()

    lax.fori_loop(0, C, end_mate, 0)
    lax.fori_loop(1, C, end_plane, 0)


def solution(mesh):
    E = mesh.shape["expert"]
    G = mesh.shape["dp"]

    def shards(tokens, routing, combine, upstream, gate_w, up_w, down_w):
        T, D = tokens.shape
        top = routing.shape[1]
        shard, F = gate_w.shape[1:]
        cap = max(T // 2, top * T // E + T // 4)
        rows = (E, cap, D)
        vmem = pl.BlockSpec(memory_space=pltpu.VMEM)
        hbm = pl.BlockSpec(memory_space=pltpu.HBM)
        results = pl.pallas_call(
            functools.partial(layer_kernel, E, G, cap),
            out_shape=(
                jax.ShapeDtypeStruct((T, D), BF),
                jax.ShapeDtypeStruct((T, D), BF),
                jax.ShapeDtypeStruct((top, T), F32),
                jax.ShapeDtypeStruct((1, shard, F), F32),
                jax.ShapeDtypeStruct((1, shard, F), F32),
            ),
            in_specs=[hbm, vmem, vmem, hbm, hbm, hbm, hbm],
            out_specs=(vmem,) * 5,
            scratch_shapes=[
                pltpu.VMEM((T, D), BF),
                pltpu.VMEM((T, D), BF),
                pltpu.VMEM((4 * top, T), F32),
                pltpu.VMEM((E, 4 * top, T), F32),
                pltpu.VMEM((2, 2, T, D), BF),
                pltpu.VMEM((2, 2, cap, D), BF),
                pltpu.VMEM((2, cap, D), BF),
                pltpu.VMEM((2, T, D), BF),
                pltpu.VMEM((T, D), BF),
                pltpu.VMEM((G * shard, 2 * F), BF),
                pltpu.VMEM((G * shard, F), BF),
            ]
            + [pltpu.VMEM(rows, BF)] * 8
            + [
                pltpu.VMEM((E, cap, 2 * F), F32),
                pltpu.VMEM((E * cap, 2 * F), BF),
                pltpu.VMEM((G, shard, 2 * F), F32),
            ]
            + [pltpu.VMEM((G // 2, shard, 2 * F), BF)] * 4
            + [
                pltpu.VMEM((shard, 2 * F), F32),
                pltpu.SemaphoreType.DMA((5,)),
                pltpu.SemaphoreType.DMA((5, E)),
                pltpu.SemaphoreType.DMA((5, E)),
            ]
            + [pltpu.SemaphoreType.DMA((2, G // 2))] * 4
            + [pltpu.SemaphoreType.DMA((G // 2,))] * 4
            + [pltpu.SemaphoreType.DMA((2,))]
            + [pltpu.SemaphoreType.DMA((2, 2))] * 3
            + [pltpu.SemaphoreType.DMA((2,))] * 4,
            compiler_params=pltpu.CompilerParams(
                collective_id=0, has_side_effects=True, vmem_limit_bytes=63 * 2**20
            ),
            cost_estimate=pl.CostEstimate(
                flops=16 * E * cap * D * F, bytes_accessed=8 * E * cap * D * 2, transcendentals=0
            ),
        )(tokens, routing.T, combine.T, upstream, gate_w, up_w, down_w)
        return (results[0], results[1], results[2].T, results[3], results[4])

    rows = P(("dp", "expert"), None)
    weights = P("expert", "dp", None)
    return jax.shard_map(
        shards,
        mesh=mesh,
        in_specs=(rows, rows, rows, rows, weights, weights, weights),
        out_specs=(rows, rows, rows, weights, weights),
        check_vma=False,
    )
```
